32 devices in a mesh: groups: 2 (over y), expert: 4 (over z), helper: 2 (over x), sub: 2 (over core).
Axes of the slice: x: 2, y: 2, z: 4, core: 2. Of those that a mesh axis runs over, the one named last changes fastest.
Arguments:
- tokens: bfloat16 [1024, 7168], P(('groups', 'expert'), ('helper', 'sub')), parts along dimension 0, may hold values from -6 to 6
- routes: int32 [1024, 8], P(('groups', 'expert')), parts along dimension 0, may hold values from 0 to 15, all different within a row; in each aligned block of 128 rows (0 to 127, 128 to 255, ...) at most 72 rows name the same one
- router_weight: bfloat16 [7168, 16], P(('helper', 'sub')), may hold values from -0.0625 to 0.0625
- gate_weight: bfloat16 [16, 7168, 2048], P('expert', None, ('helper', 'sub')), may hold values from -0.0625 to 0.0625
- up_weight: bfloat16 [16, 7168, 2048], P('expert', None, ('helper', 'sub')), may hold values from -0.0625 to 0.0625
- down_weight: bfloat16 [16, 2048, 7168], P('expert', None, ('helper', 'sub')), may hold values from -0.125 to 0.125
Outputs:
- mixed: bfloat16 [1024, 7168], P(('groups', 'expert'), ('helper', 'sub')), parts along dimension 0
- zloss: float32 [1024], P(('groups', 'expert')), parts along dimension 0
The draws below stay inside these ranges and needn't reach their ends.
There are 2 independent parts, one for each index of `groups`. The reference program is written for one: setup_inputs(seed, part) draws one part's arguments, and reference() takes and returns one part's arrays. A program takes and returns all parts, laid end to end along the dimension named above; an argument that names none is the same for every part. Nothing has to cross between parts.
Inputs may be any that keep to these rules, and one draw needn't show every extreme that they name: `routes`: in each aligned block of 128 rows (the rows of one index of the expert axis) a row names 8 different experts, no expert is named by more than 72 rows, a bound that some block reaches.
All inputs are finite; a program needn't handle non-finite values.
Results may differ from the reference program's by a relative error of at most 0.0064.
Values may be sent and summed in bfloat16 or wider, within the bound.
A program may use at most 256 MiB of HBM per device.

```python
import math
import jax
import jax.numpy as jnp
import numpy as np
from jax import lax

D = 7168
FF = 2048
TOP = 8
EXPERTS = 16
TOK_DEV = 128
CAP = 72
TOKENS = 512
N_EXPERT = 4


def level_of(stream_key, shape, split, smallest, high):
    def one(dim, shards_of):
        heights = jax.random.uniform(jax.random.fold_in(jax.random.fold_in(stream_key, 6), dim), (shards_of,), jnp.float32, smallest / len(split), high / len(split))
        return jnp.repeat(jnp.exp(heights), shape[dim] // shards_of).reshape((-1,) + (1,) * (len(shape) - dim - 1))

    level = one(*split[0])
    for cut in split[1:]:
        level = level * one(*cut)
    return level


def assign_block(key, own, number, rows, number_of, top, limit, skew):
    sequence = jax.random.permutation(key, number_of)
    heavy_load, ordinary = load_shares(number_of, rows * top, limit, skew, True), load_shares(number_of, rows * top, limit, skew, False)
    places = jnp.arange(number_of)

    def named(lengths, rotation):
        used = int((lengths > 0).sum())
        fixed = max(1, used // 4)
        passed = fixed + (places - fixed + rotation * (used - fixed)) % max(1, number_of - fixed)
        return jnp.zeros((number_of,), jnp.int32).at[sequence[jnp.where(places < fixed, places, passed)]].set(jnp.asarray(lengths, jnp.int32))

    lengths = jnp.where(number % 4 == 0, named(heavy_load, number // 4), named(ordinary, number - number // 4 - 1))
    mixed = jax.random.permutation(jax.random.fold_in(own, 3), number_of)
    donor, sink = mixed[0:number_of // 2 * 2:2], mixed[1:number_of // 2 * 2:2]
    slack = jnp.minimum(lengths[donor] - 1, limit - lengths[sink]) // 2
    slack = jnp.where((donor == sequence[0]) | (sink == sequence[0]) | (lengths[sink] == 0), 0, jnp.maximum(slack, 0))
    passed = jax.random.randint(jax.random.fold_in(own, 4), (number_of // 2,), 0, 1 << 20) % (slack + 1)
    lengths = lengths.at[donor].add(-passed).at[sink].add(passed)
    labels = jnp.searchsorted(jnp.cumsum(lengths), jnp.arange(rows * top), side="right").astype(jnp.int32)
    listing = labels.reshape(top, rows).T
    listing = listing[jax.random.permutation(jax.random.fold_in(own, 1), rows)]
    rotation = jax.random.randint(jax.random.fold_in(own, 2), (rows, 1), 0, top)
    return jnp.take_along_axis(listing, (jnp.arange(top)[None, :] + rotation) % top, axis=1)


def load_shares(count, total, bound, slope, full):
    portions = [(1 << 20) // math.isqrt(standing ** slope) + 1 for standing in range(1, count + 1)]
    largest = bound if full else min(bound, max(-(-total // count), total * portions[0] // sum(portions)))
    least = 1 if total - largest >= count - 1 else 0
    given, spare = [largest] + [least] * (count - 1), total - largest - least * (count - 1)
    while spare > 0:
        free = [i for i in range(1, count) if given[i] < largest] or [i for i in range(1, count) if given[i] < bound]
        whole, budget = sum([portions[i] for i in free]), spare
        for i in free:
            extra = min(bound - given[i], max(1, budget * portions[i] // whole), spare)
            given[i] = given[i] + extra
            spare = spare - extra
    return np.array(given)


def normal_values(rng, extent, deviation, reach, split=(), kind=jnp.bfloat16):
    array = deviation * jax.random.normal(rng, extent, jnp.float32)
    if split:
        array = array * level_of(rng, extent, split, -0.22, 0.18)
    return jnp.clip(array, -reach, reach).astype(kind)


def setup_inputs(seed: int = 0, part: int = 0) -> dict:
    arg_keys = jax.random.split(jax.random.key(seed), 7)
    own_keys = jax.random.split(jax.random.fold_in(arg_keys[6], part), 7)
    tokens = normal_values(own_keys[0], (TOKENS, D), 1.0, 6.0, ((0, 4), (1, 4)))
    routes_keys = jax.random.split(jax.random.fold_in(own_keys[1], 1), TOKENS // TOK_DEV)
    routes_turns = jax.random.permutation(jax.random.fold_in(own_keys[1], 3), TOKENS // TOK_DEV)
    routes = jax.vmap(lambda own, number: assign_block(jax.random.fold_in(own_keys[1], 2), own, number, TOK_DEV, EXPERTS, TOP, CAP, 2))(routes_keys, routes_turns).reshape((TOKENS, TOP))
    router_weight = normal_values(arg_keys[2], (D, EXPERTS), D ** -0.5, 0.0625, ((0, 4),))
    gate_weight = normal_values(arg_keys[3], (EXPERTS, D, FF), D ** -0.5, 0.0625, ((0, 4), (2, 4)))
    up_weight = normal_values(arg_keys[4], (EXPERTS, D, FF), D ** -0.5, 0.0625, ((0, 4), (2, 4)))
    down_weight = normal_values(arg_keys[5], (EXPERTS, FF, D), FF ** -0.5, 0.125, ((0, 4), (2, 4)))
    return dict(tokens=tokens, routes=routes, router_weight=router_weight, gate_weight=gate_weight, up_weight=up_weight, down_weight=down_weight)


def slot_of(block_routes, count, capacity):
    flat = block_routes.reshape(-1).astype(jnp.int32)
    table = (flat[:, None] == jnp.arange(count, dtype=jnp.int32)[None, :]).astype(jnp.int32)
    before = (jnp.cumsum(table, axis=0) - table).astype(jnp.int32)
    place = jnp.sum(before * table, axis=1).astype(jnp.int32)
    return (flat * capacity + place).astype(jnp.int32)


def source_of(slots, rows, top, count, capacity):
    owner = (jnp.arange(rows * top, dtype=jnp.int32) // top).astype(jnp.int32)
    return jnp.full((count * capacity,), rows, jnp.int32).at[slots].set(owner)


def run_expert(operands):
    rows, gate_w, up_w, down_w = operands
    gate = jnp.dot(rows, gate_w, preferred_element_type=jnp.float32)
    up = jnp.dot(rows, up_w, preferred_element_type=jnp.float32)
    hidden = (jax.nn.silu(gate) * up).astype(jnp.bfloat16)
    return jnp.dot(hidden, down_w, preferred_element_type=jnp.float32).astype(jnp.bfloat16)


def reference(tokens, routes, router_weight, gate_weight, up_weight, down_weight):
    logits = jnp.dot(tokens, router_weight, preferred_element_type=jnp.float32)
    zloss = jnp.square(jnp.log(jnp.sum(jnp.exp(logits), axis=1)))
    chosen = jnp.take_along_axis(logits, routes.astype(jnp.int32), axis=1)
    affinity = jax.nn.sigmoid(chosen)
    gates = (2.5 * affinity / jnp.sum(affinity, axis=1, keepdims=True)).astype(jnp.bfloat16)
    blocks = tokens.reshape(N_EXPERT, TOK_DEV, D)
    block_routes = routes.reshape(N_EXPERT, TOK_DEV, TOP)
    slots = jax.vmap(lambda r: slot_of(r, EXPERTS, CAP))(block_routes)
    sources = jax.vmap(lambda s: source_of(s, TOK_DEV, TOP, EXPERTS, CAP))(slots)
    padded = jnp.concatenate([blocks, jnp.zeros((N_EXPERT, 1, D), jnp.bfloat16)], axis=1)
    buffers = jax.vmap(lambda p, s: p[s])(padded, sources)
    per_expert = buffers.reshape(N_EXPERT, EXPERTS, CAP, D).transpose(1, 0, 2, 3).reshape(EXPERTS, N_EXPERT * CAP, D)
    answers = lax.map(run_expert, (per_expert, gate_weight, up_weight, down_weight))
    back = answers.reshape(EXPERTS, N_EXPERT, CAP, D).transpose(1, 0, 2, 3).reshape(N_EXPERT, EXPERTS * CAP, D)
    picked = jax.vmap(lambda b, s: b[s])(back, slots).reshape(TOKENS, TOP, D)
    mixed = jnp.einsum("tk,tkd->td", gates.astype(jnp.float32), picked.astype(jnp.float32))
    return mixed.astype(jnp.bfloat16), zloss
```

```python
import functools

import jax
import jax.numpy as jnp
from jax import lax
from jax.experimental import pallas as pl
from jax.experimental.pallas import tpu as pltpu
from jax.sharding import PartitionSpec as P

CAP = 72
CHUNKS = 7
AHEAD = 2
SLOTS = 2
MESH = pl.DeviceIdType.MESH
F32 = jnp.float32
BF16 = jnp.bfloat16


def barrier_all(axes):
    sem = pltpu.get_barrier_semaphore()
    total = 0
    for name in axes:
        size = lax.axis_size(name)
        me = lax.axis_index(name)
        for d in range(1, size):
            pl.semaphore_signal(
                sem, inc=1, device_id={name: lax.rem(me + d, size)}, device_id_type=MESH
            )
            total += 1
    pl.semaphore_wait(sem, total)


def dispatch_kernel(
    dims, tok_ref, routes_ref, gate_hbm, up_hbm, hid_ref, rank_ref,
    tokbuf, wbuf, rows, acc, places,
    recv, send_z, send_x, send_s, w_sem, r_send, r_recv,
):
    n, h, s, local, chunks, width, ff, experts = dims
    z, x, c = lax.axis_index("expert"), lax.axis_index("helper"), lax.axis_index("sub")
    other = 1 - c
    q_own = x * s + c
    toks = tok_ref.shape[0]

    def weights(k, slot):
        return (
            pltpu.make_async_copy(gate_hbm.at[:, :, k], wbuf.at[slot, 0], w_sem.at[slot, 0]),
            pltpu.make_async_copy(up_hbm.at[:, :, k], wbuf.at[slot, 1], w_sem.at[slot, 1]),
        )

    def copy(k, q, zz, send, target):
        return pltpu.make_async_remote_copy(
            src_ref=tokbuf.at[k, q, zz], dst_ref=tokbuf.at[k, q, zz],
            send_sem=send, recv_sem=recv.at[k, q, zz],
            device_id=target, device_id_type=MESH,
        )

    def to_z(k, d):
        return copy(k, q_own, z, send_z.at[k, d - 1], {"expert": lax.rem(z + d, n)})

    def to_x(k, zz, d):
        return copy(k, q_own, zz, send_x.at[k, zz, d - 1], {"helper": lax.rem(x + d, h)})

    def to_s(k, xx, zz):
        return copy(k, xx * s + c, zz, send_s.at[k, xx, zz], {"sub": other})

    def rank_copy(d):
        return pltpu.make_async_remote_copy(
            src_ref=rank_ref.at[z], dst_ref=rank_ref.at[z],
            send_sem=r_send.at[d - 1], recv_sem=r_recv.at[z],
            device_id={"expert": lax.rem(z + d, n)}, device_id_type=MESH,
        )

    def own(k):
        for d in range(1, n):
            to_z(k, d).start()
        for d in range(1, h):
            to_x(k, z, d).start()
        to_s(k, x, z).start()

    for k in range(SLOTS):
        for w in weights(k, k):
            w.start()
    for k in range(chunks):
        tokbuf[k, q_own, z] = tok_ref[:, k * width:(k + 1) * width]

    ids = lax.broadcasted_iota(jnp.int32, (toks, experts), 1)
    named = jnp.zeros((toks, experts), F32)
    for k in range(routes_ref.shape[1]):
        named = named + jnp.where(routes_ref[:, k:k + 1] == ids, 1.0, 0.0)
    before = lax.broadcasted_iota(jnp.int32, (toks, toks), 0) < lax.broadcasted_iota(jnp.int32, (toks, toks), 1)
    same = lax.broadcasted_iota(jnp.int32, (toks, toks), 0) == lax.broadcasted_iota(jnp.int32, (toks, toks), 1)
    over = (((0,), (0,)), ((), ()))
    earlier = lax.dot_general(named, jnp.where(before, 1.0, 0.0), over, preferred_element_type=F32)
    chosen = lax.dot_general(named, jnp.where(same, 1.0, 0.0), over, preferred_element_type=F32)
    rank_ref[z] = jnp.where(chosen > 0.5, earlier, -1.0)

    barrier_all(("expert", "helper", "sub"))
    for d in range(1, n):
        rank_copy(d).start()
    for k in range(min(AHEAD, chunks)):
        own(k)

    acc[...] = jnp.zeros_like(acc)
    for d in range(1, n):
        zz = lax.rem(z + n - d, n)
        pltpu.make_async_remote_copy(
            src_ref=rank_ref.at[zz], dst_ref=rank_ref.at[zz], send_sem=r_send.at[0],
            recv_sem=r_recv.at[zz], device_id={"sub": other}, device_id_type=MESH,
        ).wait_recv()
    slot_ids = lax.broadcasted_iota(jnp.int32, (CAP, toks), 0).astype(F32)
    for b in range(n):
        for l in range(local):
            line = rank_ref[b, pl.ds(z * local + l, 1), :]
            places[b, l * CAP:(l + 1) * CAP, :] = jnp.where(slot_ids == line, 1.0, 0.0)

    def compute(k):
        slot = lax.rem(k, SLOTS)
        for q in range(h * s):
            parts = []
            for b in range(n):
                parts.append(
                    jnp.dot(places[b].astype(BF16), tokbuf[k, q, b], preferred_element_type=F32)
                )
            for l in range(local):
                stack = jnp.concatenate([p[l * CAP:(l + 1) * CAP] for p in parts], axis=0)
                rows[l, :, q * width:(q + 1) * width] = stack.astype(BF16)
        for w in weights(k, slot):
            w.wait()

        def one(l, carry):
            for m in range(2):
                acc[m, l] += jnp.dot(
                    rows[l], wbuf[slot, m, l].reshape(h * s * width, ff), preferred_element_type=F32
                )
            return carry

        lax.fori_loop(0, local, one, 0)

        @pl.when(k + SLOTS < chunks)
        def _():
            for w in weights(k + SLOTS, slot):
                w.start()

    def step(t, carry):
        @pl.when(t + AHEAD < chunks)
        def _():
            own(t + AHEAD)

        @pl.when(t < chunks)
        def _():
            for d in range(1, n):
                zz = lax.rem(z + n - d, n)
                copy(t, q_own, zz, send_z.at[t, 0], {"sub": other}).wait_recv()
                for e in range(1, h):
                    to_x(t, zz, e).start()
                to_s(t, x, zz).start()

        @pl.when((t >= 1) & (t <= chunks))
        def _():
            k = t - 1
            for d in range(0, n):
                zz = lax.rem(z + n - d, n)
                for e in range(1, h):
                    xx = lax.rem(x + e, h)
                    copy(k, xx * s + c, zz, send_z.at[k, 0], {"sub": other}).wait_recv()
                    to_s(k, xx, zz).start()

        @pl.when(t >= 2)
        def _():
            k = t - 2
            for zz in range(n):
                for xx in range(h):
                    copy(k, xx * s + other, zz, send_z.at[k, 0], {"sub": other}).wait_recv()
            compute(k)

        return carry

    lax.fori_loop(0, chunks + 2, step, 0)

    def finish(l, carry):
        gate = acc[0, l]
        hid_ref[l] = (gate / (1.0 + jnp.exp(-gate)) * acc[1, l]).astype(BF16)
        return carry

    lax.fori_loop(0, local, finish, 0)

    def drain(k, carry):
        for d in range(1, n):
            to_z(k, d).wait_send()
        for zz in range(n):
            for d in range(1, h):
                to_x(k, zz, d).wait_send()
            for xx in range(h):
                to_s(k, xx, zz).wait_send()
        return carry

    lax.fori_loop(0, chunks, drain, 0)
    for d in range(1, n):
        rank_copy(d).wait_send()


def dispatch(tokens, routes, gate_weight, up_weight, experts):
    n, h, s = (lax.axis_size(a) for a in ("expert", "helper", "sub"))
    local, wide, ff = gate_weight.shape
    toks, own = tokens.shape
    width = own // CHUNKS
    shape = (local, h * s, CHUNKS, width, ff)
    dims = (n, h, s, local, CHUNKS, width, ff, experts)
    dma = pltpu.SemaphoreType.DMA
    vmem = pl.BlockSpec(memory_space=pltpu.VMEM)
    hbm = pl.BlockSpec(memory_space=pl.ANY)
    return pl.pallas_call(
        functools.partial(dispatch_kernel, dims),
        out_shape=(
            jax.ShapeDtypeStruct((local, n * CAP, ff), BF16),
            jax.ShapeDtypeStruct((n, experts, toks), F32),
        ),
        in_specs=[vmem, vmem, hbm, hbm],
        out_specs=(vmem, vmem),
        scratch_shapes=[
            pltpu.VMEM((CHUNKS, h * s, n, toks, width), BF16),
            pltpu.VMEM((SLOTS, 2, local, h * s, width, ff), BF16),
            pltpu.VMEM((local, n * CAP, h * s * width), BF16),
            pltpu.VMEM((2, local, n * CAP, ff), F32),
            pltpu.VMEM((n, local * CAP, toks), F32),
            dma((CHUNKS, h * s, n)),
            dma((CHUNKS, max(n - 1, 1))),
            dma((CHUNKS, n, max(h - 1, 1))),
            dma((CHUNKS, h, n)),
            dma((SLOTS, 2)),
            dma((max(n - 1, 1),)),
            dma((n,)),
        ],
        compiler_params=pltpu.CompilerParams(
            collective_id=0, has_side_effects=True, vmem_limit_bytes=60 * 1024 * 1024
        ),
        cost_estimate=pl.CostEstimate(
            flops=4 * local * n * CAP * wide * ff,
            bytes_accessed=4 * local * wide * ff,
            transcendentals=local * n * CAP * ff,
        ),
        name="dispatch_up",
    )(tokens, routes, gate_weight.reshape(shape), up_weight.reshape(shape))


def body(tokens, routes, router_weight, gate_weight, up_weight, down_weight):
    toks = tokens.shape[0]
    experts = router_weight.shape[1]
    n = lax.axis_size("expert")
    local = gate_weight.shape[0]
    partial_logits = jnp.dot(tokens, router_weight, preferred_element_type=F32)
    logits = lax.psum(partial_logits, ("helper", "sub"))
    zloss = jnp.square(jnp.log(jnp.sum(jnp.exp(logits), axis=1)))
    named = jnp.any(routes[:, :, None] == jnp.arange(experts, dtype=jnp.int32), axis=1)
    affinity = jnp.where(named, jax.nn.sigmoid(logits), 0.0)
    gates = (2.5 * affinity / jnp.sum(affinity, axis=1, keepdims=True)).astype(BF16)
    all_gates = lax.all_gather(gates.T, "expert", axis=0)
    hidden, ranks = dispatch(tokens, routes, gate_weight, up_weight, experts)
    home = lax.axis_index("expert") * local
    my_ranks = lax.dynamic_slice_in_dim(ranks, home, local, 1)
    my_gates = lax.dynamic_slice_in_dim(all_gates, home, local, 1)
    slot_ids = jnp.arange(CAP, dtype=F32)[None, None, :, None]
    table = jnp.where(my_ranks[:, :, None, :] == slot_ids, my_gates[:, :, None, :], 0.0).astype(BF16)
    full = lax.all_gather(hidden, ("helper", "sub"), axis=2, tiled=True)
    answer = jnp.einsum("lrf,lfd->lrd", full, down_weight, preferred_element_type=F32).astype(BF16)
    answer = answer.reshape(local, n, CAP, -1)
    part = jnp.einsum("blct,lbcd->btd", table, answer, preferred_element_type=F32).astype(BF16)
    pieces = lax.all_to_all(part, "expert", split_axis=0, concat_axis=0, tiled=True)
    mixed = jnp.sum(pieces.astype(F32), axis=0)
    return (mixed.astype(BF16), zloss)


def solution(mesh):
    placed = (
        P(("groups", "expert"), ("helper", "sub")),
        P(("groups", "expert"), None),
        P(("helper", "sub"), None),
        P("expert", None, ("helper", "sub")),
        P("expert", None, ("helper", "sub")),
        P("expert", None, ("helper", "sub")),
    )
    return jax.shard_map(
        body,
        mesh=mesh,
        in_specs=placed,
        out_specs=(P(("groups", "expert"), ("helper", "sub")), P(("groups", "expert"))),
        check_vma=False,
    )
```

```python
import functools

import jax
import jax.numpy as jnp
from jax import lax
from jax.experimental import pallas as pl
from jax.experimental.pallas import tpu as pltpu
from jax.sharding import PartitionSpec as P

CAP = 72
CHUNKS = 7
AHEAD = 2
SLOTS = 2
D_SLOTS = 2
VMEM_LIMIT = 62 * 1024 * 1024
MESH = pl.DeviceIdType.MESH
F32 = jnp.float32
BF16 = jnp.bfloat16


def layer_kernel(
    dims, tok_ref, routes_ref, router_ref, gate_hbm, up_hbm, down_hbm, out_ref, zloss_ref,
    tokbuf, wbuf, dbuf, rows, acc, places, table, ranks, gates, logits, hbuf, part, sendbuf, recvbuf,
    recv, send_z, send_x, send_s, w_sem, d_sem, r_send, r_recv, g_send, g_recv, l_send, l_recv,
    h_recv, h_send_x, h_send_s, p_send, p_recv,
):
    n, h, s, local, chunks, width, ff, experts, d_slots = dims
    z, x, c = lax.axis_index("expert"), lax.axis_index("helper"), lax.axis_index("sub")
    other = 1 - c
    q_own = x * s + c
    toks = tok_ref.shape[0]
    nh = n // 2
    half = nh * CAP
    items = 2 * local

    def weights(k, slot):
        return (
            pltpu.make_async_copy(gate_hbm.at[:, :, k], wbuf.at[slot, 0], w_sem.at[slot, 0]),
            pltpu.make_async_copy(up_hbm.at[:, :, k], wbuf.at[slot, 1], w_sem.at[slot, 1]),
        )

    def down(l, slot):
        return pltpu.make_async_copy(down_hbm.at[l], dbuf.at[slot], d_sem.at[slot])

    def remote(src, dst, send, got, target):
        return pltpu.make_async_remote_copy(
            src_ref=src, dst_ref=dst, send_sem=send, recv_sem=got,
            device_id=target, device_id_type=MESH,
        )

    def copy(k, q, zz, send, target):
        ref = tokbuf.at[k, q, zz]
        return remote(ref, ref, send, recv.at[k, q, zz], target)

    def to_z(k, d):
        return copy(k, q_own, z, send_z.at[k, d - 1], {"expert": lax.rem(z + d, n)})

    def to_x(k, zz, d):
        return copy(k, q_own, zz, send_x.at[k, zz, d - 1], {"helper": lax.rem(x + d, h)})

    def to_s(k, xx, zz):
        return copy(k, xx * s + c, zz, send_s.at[k, xx, zz], {"sub": other})

    def rank_copy(d):
        ref = ranks.at[z]
        return remote(ref, ref, r_send.at[d - 1], r_recv.at[z], {"expert": lax.rem(z + d, n)})

    def gate_copy(d):
        ref = gates.at[z]
        return remote(ref, ref, g_send.at[d - 1], g_recv.at[z], {"expert": lax.rem(z + d, n)})

    def logit_copy(d, e):
        ref = logits.at[q_own]
        target = {"helper": lax.rem(x + d, h), "sub": lax.rem(c + e, s)}
        return remote(ref, ref, l_send.at[d, e], l_recv.at[q_own], target)

    peers = [(d, e) for d in range(h) for e in range(s) if d or e]

    def hid_copy(f, l, q, send, target):
        ref = hbuf.at[f, l, q]
        return remote(ref, ref, send, h_recv.at[f, l, q], target)

    def hid_x(f, l, d):
        return hid_copy(f, l, q_own, h_send_x.at[f, l, d - 1], {"helper": lax.rem(x + d, h)})

    def hid_s(f, l, xx):
        return hid_copy(f, l, xx * s + c, h_send_s.at[f, l, xx], {"sub": other})

    def hid_start(f, l):
        for d in range(1, h):
            hid_x(f, l, d).start()
        hid_s(f, l, x).start()

    def back(p):
        return remote(
            sendbuf.at[p], recvbuf.at[p], p_send.at[p], p_recv.at[p],
            {"expert": lax.rem(z + 1 + p, n)},
        )

    def own(k):
        for d in range(1, n):
            to_z(k, d).start()
        for d in range(1, h):
            to_x(k, z, d).start()
        to_s(k, x, z).start()

    for k in range(SLOTS):
        for w in weights(k, k):
            w.start()
    for l in range(min(local, d_slots)):
        down(l, l).start()
    for k in range(chunks):
        tokbuf[k, q_own, z] = tok_ref[:, k * width:(k + 1) * width]

    ids = lax.broadcasted_iota(jnp.int32, (toks, experts), 1)
    named = jnp.zeros((toks, experts), F32)
    for k in range(routes_ref.shape[1]):
        named = named + jnp.where(routes_ref[:, k:k + 1] == ids, 1.0, 0.0)
    before = lax.broadcasted_iota(jnp.int32, (toks, toks), 0) < lax.broadcasted_iota(jnp.int32, (toks, toks), 1)
    same = lax.broadcasted_iota(jnp.int32, (toks, toks), 0) == lax.broadcasted_iota(jnp.int32, (toks, toks), 1)
    over = (((0,), (0,)), ((), ()))
    earlier = lax.dot_general(named, jnp.where(before, 1.0, 0.0), over, preferred_element_type=F32)
    chosen = lax.dot_general(named, jnp.where(same, 1.0, 0.0), over, preferred_element_type=F32)
    ranks[z] = jnp.where(chosen > 0.5, earlier, -1.0)
    mine = jnp.dot(tok_ref[...], router_ref[...], preferred_element_type=F32)
    mine = jnp.concatenate([mine, jnp.zeros((toks, 128 - experts), F32)], axis=1)
    logits[q_own] = mine.T[:experts]

    sem = pltpu.get_barrier_semaphore()
    for d in range(1, n):
        pl.semaphore_signal(sem, inc=1, device_id={"expert": lax.rem(z + d, n)}, device_id_type=MESH)
    for d, e in peers:
        target = {"helper": lax.rem(x + d, h), "sub": lax.rem(c + e, s)}
        pl.semaphore_signal(sem, inc=1, device_id=target, device_id_type=MESH)
    pl.semaphore_wait(sem, n - 1 + len(peers))

    for d, e in peers:
        logit_copy(d, e).start()
    for d in range(1, n):
        rank_copy(d).start()
    for k in range(min(AHEAD, chunks)):
        own(k)

    acc[...] = jnp.zeros_like(acc)
    part[...] = jnp.zeros_like(part)
    for d, e in peers:
        q = lax.rem(x + d, h) * s + lax.rem(c + e, s)
        remote(logits.at[q], logits.at[q], l_send.at[0, 0], l_recv.at[q], {"sub": other}).wait_recv()
    total = logits[0]
    for q in range(1, h * s):
        total = total + logits[q]
    zloss_ref[...] = jnp.square(jnp.log(jnp.sum(jnp.exp(total), axis=0, keepdims=True)))
    affinity = jnp.where(ranks[z] >= 0.0, 1.0 / (1.0 + jnp.exp(-total)), 0.0)
    gates[z] = (2.5 * affinity / jnp.sum(affinity, axis=0, keepdims=True)).astype(BF16).astype(F32)
    for d in range(1, n):
        gate_copy(d).start()
    for d in range(1, n):
        zz = lax.rem(z + n - d, n)
        remote(ranks.at[zz], ranks.at[zz], r_send.at[0], r_recv.at[zz], {"sub": other}).wait_recv()
    slot_ids = lax.broadcasted_iota(jnp.int32, (CAP, toks), 0).astype(F32)
    for b in range(n):
        for l in range(local):
            line = ranks[b, pl.ds(z * local + l, 1), :]
            places[b, l * CAP:(l + 1) * CAP, :] = jnp.where(slot_ids == line, 1.0, 0.0)

    def compute(k):
        slot = lax.rem(k, SLOTS)
        for q in range(h * s):
            parts = []
            for p in range(n):
                b = lax.rem(z + 1 + p, n)
                parts.append(
                    jnp.dot(places[b].astype(BF16), tokbuf[k, q, b], preferred_element_type=F32)
                )
            for l in range(local):
                stack = jnp.concatenate([p[l * CAP:(l + 1) * CAP] for p in parts], axis=0)
                rows[l, :, q * width:(q + 1) * width] = stack.astype(BF16)
        for w in weights(k, slot):
            w.wait()

        def one(l, carry):
            for m in range(2):
                acc[m, l] += jnp.dot(
                    rows[l], wbuf[slot, m, l].reshape(h * s * width, ff), preferred_element_type=F32
                )

            @pl.when(k == chunks - 1)
            def _():
                for f in range(2):
                    gate = acc[0, l, f * half:(f + 1) * half]
                    up = acc[1, l, f * half:(f + 1) * half]
                    hbuf[f, l, q_own] = (gate / (1.0 + jnp.exp(-gate)) * up).astype(BF16)
                hid_start(0, l)

            return carry

        lax.fori_loop(0, local, one, 0)

        @pl.when(k + SLOTS < chunks)
        def _():
            for w in weights(k + SLOTS, slot):
                w.start()

    def step(t, carry):
        @pl.when(t + AHEAD < chunks)
        def _():
            own(t + AHEAD)

        @pl.when(t < chunks)
        def _():
            for d in range(1, n):
                zz = lax.rem(z + n - d, n)
                copy(t, q_own, zz, send_z.at[t, 0], {"sub": other}).wait_recv()
                for e in range(1, h):
                    to_x(t, zz, e).start()
                to_s(t, x, zz).start()

        @pl.when((t >= 1) & (t <= chunks))
        def _():
            k = t - 1
            for d in range(0, n):
                zz = lax.rem(z + n - d, n)
                for e in range(1, h):
                    xx = lax.rem(x + e, h)
                    copy(k, xx * s + c, zz, send_z.at[k, 0], {"sub": other}).wait_recv()
                    to_s(k, xx, zz).start()

        @pl.when(t >= 2)
        def _():
            k = t - 2
            for zz in range(n):
                for xx in range(h):
                    copy(k, xx * s + other, zz, send_z.at[k, 0], {"sub": other}).wait_recv()
            compute(k)

        return carry

    lax.fori_loop(0, chunks + 2, step, 0)
    for l in range(local):
        hid_start(1, l)

    for d in range(1, n):
        zz = lax.rem(z + n - d, n)
        remote(gates.at[zz], gates.at[zz], g_send.at[0], g_recv.at[zz], {"sub": other}).wait_recv()
    blank = jnp.zeros((CAP, toks), F32)
    padded = -(-half // 128) * 128
    for f in range(2):
        for l in range(local):
            lines = []
            for i in range(nh):
                b = lax.rem(z + 1 + f * nh + i, n)
                at = pl.ds(z * local + l, 1)
                block = jnp.where(slot_ids == ranks[b, at, :], gates[b, at, :], 0.0)
                lines.append(jnp.concatenate([block if j == i else blank for j in range(nh)], axis=1))
            if padded > half:
                lines.append(jnp.zeros((padded - half, nh * toks), F32))
            table[f, l] = jnp.concatenate(lines, axis=0).T[:, :half].astype(BF16)

    def hid_forward(i):
        f, l = i // local, lax.rem(i, local)
        for e in range(1, h):
            xx = lax.rem(x + e, h)
            hid_copy(f, l, xx * s + c, h_send_x.at[f, l, 0], {"sub": other}).wait_recv()
            hid_s(f, l, xx).start()

    hid_forward(jnp.int32(0))

    def item(i, carry):
        f, l = i // local, lax.rem(i, local)

        @pl.when(i + 1 < items)
        def _():
            hid_forward(i + 1)

        for xx in range(h):
            hid_copy(f, l, xx * s + other, h_send_x.at[f, l, 0], {"sub": other}).wait_recv()
        slot = lax.rem(i, d_slots)
        if local > d_slots:
            down(l, slot).wait()
        else:
            @pl.when(i < local)
            def _():
                down(l, slot).wait()

        def column(j, inner):
            cols = pl.ds(pl.multiple_of(j * width, width), width)
            answer = jnp.zeros((half, width), F32)
            for q in range(h * s):
                answer = answer + jnp.dot(
                    hbuf[f, l, q], dbuf[slot, q * ff:(q + 1) * ff, cols], preferred_element_type=F32
                )
            part[f, :, cols] += jnp.dot(table[f, l], answer.astype(BF16), preferred_element_type=F32)
            return inner

        lax.fori_loop(0, chunks, column, 0)
        if local > d_slots:
            @pl.when(i + d_slots < items)
            def _():
                down(lax.rem(i + d_slots, local), slot).start()

        for f_done in range(2):
            @pl.when(i == (f_done + 1) * local - 1)
            def _():
                for p in range(f_done * nh, min((f_done + 1) * nh, n - 1)):
                    at = (p - f_done * nh) * toks
                    sendbuf[p] = part[f_done, at:at + toks].astype(BF16)
                    back(p).start()

        return carry

    lax.fori_loop(0, items, item, 0)

    for p in range(n - 1):
        back(p).wait_recv()
    result = part[1, (nh - 1) * toks:]
    for p in range(n - 1):
        result = result + recvbuf[p].astype(F32)
    out_ref[...] = result.astype(BF16)

    def drain(k, carry):
        for d in range(1, n):
            to_z(k, d).wait_send()
        for zz in range(n):
            for d in range(1, h):
                to_x(k, zz, d).wait_send()
            for xx in range(h):
                to_s(k, xx, zz).wait_send()
        return carry

    lax.fori_loop(0, chunks, drain, 0)

    def drain_hidden(l, carry):
        for f in range(2):
            for d in range(1, h):
                hid_x(f, l, d).wait_send()
            for xx in range(h):
                hid_s(f, l, xx).wait_send()
        return carry

    lax.fori_loop(0, local, drain_hidden, 0)
    for d in range(1, n):
        rank_copy(d).wait_send()
        gate_copy(d).wait_send()
        back(d - 1).wait_send()
    for d, e in peers:
        logit_copy(d, e).wait_send()


def body(tokens, routes, router_weight, gate_weight, up_weight, down_weight):
    n, h, s = (lax.axis_size(a) for a in ("expert", "helper", "sub"))
    experts = router_weight.shape[1]
    local, wide, ff = gate_weight.shape
    toks, own = tokens.shape
    width = own // CHUNKS
    q = h * s
    half = n // 2 * CAP
    shape = (local, q, CHUNKS, width, ff)
    d_slots = min(local, D_SLOTS)
    dims = (n, h, s, local, CHUNKS, width, ff, experts, d_slots)
    dma = pltpu.SemaphoreType.DMA
    vmem = pl.BlockSpec(memory_space=pltpu.VMEM)
    hbm = pl.BlockSpec(memory_space=pl.ANY)
    mixed, zloss = pl.pallas_call(
        functools.partial(layer_kernel, dims),
        out_shape=(
            jax.ShapeDtypeStruct((toks, own), BF16),
            jax.ShapeDtypeStruct((1, toks), F32),
        ),
        in_specs=[vmem, vmem, vmem, hbm, hbm, hbm],
        out_specs=(vmem, vmem),
        scratch_shapes=[
            pltpu.VMEM((CHUNKS, q, n, toks, width), BF16),
            pltpu.VMEM((SLOTS, 2, local, q, width, ff), BF16),
            pltpu.VMEM((d_slots, q * ff, own), BF16),
            pltpu.VMEM((local, n * CAP, q * width), BF16),
            pltpu.VMEM((2, local, n * CAP, ff), F32),
            pltpu.VMEM((n, local * CAP, toks), F32),
            pltpu.VMEM((2, local, n // 2 * toks, half), BF16),
            pltpu.VMEM((n, experts, toks), F32),
            pltpu.VMEM((n, experts, toks), F32),
            pltpu.VMEM((q, experts, toks), F32),
            pltpu.VMEM((2, local, q, half, ff), BF16),
            pltpu.VMEM((2, n // 2 * toks, own), F32),
            pltpu.VMEM((n - 1, toks, own), BF16),
            pltpu.VMEM((n - 1, toks, own), BF16),
            dma((CHUNKS, q, n)),
            dma((CHUNKS, n - 1)),
            dma((CHUNKS, n, h - 1)),
            dma((CHUNKS, h, n)),
            dma((SLOTS, 2)),
            dma((d_slots,)),
            dma((n - 1,)),
            dma((n,)),
            dma((n - 1,)),
            dma((n,)),
            dma((h, s)),
            dma((q,)),
            dma((2, local, q)),
            dma((2, local, h - 1)),
            dma((2, local, h)),
            dma((n - 1,)),
            dma((n - 1,)),
        ],
        compiler_params=pltpu.CompilerParams(
            collective_id=0, has_side_effects=True, vmem_limit_bytes=VMEM_LIMIT
        ),
        cost_estimate=pl.CostEstimate(
            flops=6 * local * n * CAP * wide * ff,
            bytes_accessed=6 * local * wide * ff,
            transcendentals=local * n * CAP * ff,
        ),
        name="expert_layer",
    )(
        tokens, routes, router_weight,
        gate_weight.reshape(shape), up_weight.reshape(shape), down_weight,
    )
    return mixed, zloss.reshape(toks)


def solution(mesh):
    placed = (
        P(("groups", "expert"), ("helper", "sub")),
        P(("groups", "expert"), None),
        P(("helper", "sub"), None),
        P("expert", None, ("helper", "sub")),
        P("expert", None, ("helper", "sub")),
        P("expert", None, ("helper", "sub")),
    )
    return jax.shard_map(
        body,
        mesh=mesh,
        in_specs=placed,
        out_specs=(P(("groups", "expert"), ("helper", "sub")), P(("groups", "expert"))),
        check_vma=False,
    )
```

```python
import functools

import jax
import jax.numpy as jnp
from jax import lax
from jax.experimental import pallas as pl
from jax.experimental.pallas import tpu as pltpu
from jax.sharding import PartitionSpec as P

CAP = 72
CHUNKS = 7
AHEAD = 2
SLOTS = 2
D_SLOTS = 2
VMEM_LIMIT = 62 * 1024 * 1024
MESH = pl.DeviceIdType.MESH
F32 = jnp.float32
BF16 = jnp.bfloat16


def layer_kernel(
    dims, tok_ref, routes_ref, router_ref, gate_hbm, up_hbm, down_hbm, out_ref, zloss_ref,
    tokbuf, wbuf, dbuf, rows, acc, places, table, ranks, gates, logits, hbuf, part, sendbuf, recvbuf,
    recv, send_z, send_x, send_s, w_sem, d_sem, r_send, r_recv, g_send, g_recv, l_send, l_recv,
    h_recv, h_send_x, h_send_s, p_send, p_recv,
):
    n, h, s, local, chunks, width, ff, experts, d_slots = dims
    z, x, c = lax.axis_index("expert"), lax.axis_index("helper"), lax.axis_index("sub")
    other = 1 - c
    q_own = x * s + c
    toks = tok_ref.shape[0]
    nh = n // 2
    half = nh * CAP
    items = 2 * local

    def weights(k, slot):
        return (
            pltpu.make_async_copy(gate_hbm.at[:, :, k], wbuf.at[slot, 0], w_sem.at[slot, 0]),
            pltpu.make_async_copy(up_hbm.at[:, :, k], wbuf.at[slot, 1], w_sem.at[slot, 1]),
        )

    def down(l, slot):
        return pltpu.make_async_copy(down_hbm.at[l], dbuf.at[slot], d_sem.at[slot])

    def remote(src, dst, send, got, target):
        return pltpu.make_async_remote_copy(
            src_ref=src, dst_ref=dst, send_sem=send, recv_sem=got,
            device_id=target, device_id_type=MESH,
        )

    def copy(k, q, zz, send, target):
        ref = tokbuf.at[k, q, zz]
        return remote(ref, ref, send, recv.at[k, q, zz], target)

    def to_z(k, d):
        return copy(k, q_own, z, send_z.at[k, d - 1], {"expert": lax.rem(z + d, n)})

    def to_x(k, zz, d):
        return copy(k, q_own, zz, send_x.at[k, zz, d - 1], {"helper": lax.rem(x + d, h)})

    def to_s(k, xx, zz):
        return copy(k, xx * s + c, zz, send_s.at[k, xx, zz], {"sub": other})

    def rank_copy(d):
        ref = ranks.at[z]
        return remote(ref, ref, r_send.at[d - 1], r_recv.at[z], {"expert": lax.rem(z + d, n)})

    def gate_copy(d):
        ref = gates.at[z]
        return remote(ref, ref, g_send.at[d - 1], g_recv.at[z], {"expert": lax.rem(z + d, n)})

    def logit_copy(d, e):
        ref = logits.at[q_own]
        target = {"helper": lax.rem(x + d, h), "sub": lax.rem(c + e, s)}
        return remote(ref, ref, l_send.at[d, e], l_recv.at[q_own], target)

    peers = [(d, e) for d in range(h) for e in range(s) if d or e]

    def hid_copy(f, l, q, send, target):
        ref = hbuf.at[f, l, q]
        return remote(ref, ref, send, h_recv.at[f, l, q], target)

    def hid_x(f, l, d):
        return hid_copy(f, l, q_own, h_send_x.at[f, l, d - 1], {"helper": lax.rem(x + d, h)})

    def hid_s(f, l, xx):
        return hid_copy(f, l, xx * s + c, h_send_s.at[f, l, xx], {"sub": other})

    def hid_start(f, l):
        for d in range(1, h):
            hid_x(f, l, d).start()
        hid_s(f, l, x).start()

    def back(p):
        return remote(
            sendbuf.at[p], recvbuf.at[p], p_send.at[p], p_recv.at[p],
            {"expert": lax.rem(z + 1 + p, n)},
        )

    def own(k):
        for d in range(1, n):
            to_z(k, d).start()
        for d in range(1, h):
            to_x(k, z, d).start()
        to_s(k, x, z).start()

    for k in range(SLOTS):
        for w in weights(k, k):
            w.start()
    for l in range(min(local, d_slots)):
        down(l, l).start()
    for k in range(chunks):
        tokbuf[k, q_own, z] = tok_ref[:, k * width:(k + 1) * width]

    ids = lax.broadcasted_iota(jnp.int32, (toks, experts), 1)
    named = jnp.zeros((toks, experts), F32)
    for k in range(routes_ref.shape[1]):
        named = named + jnp.where(routes_ref[:, k:k + 1] == ids, 1.0, 0.0)
    before = lax.broadcasted_iota(jnp.int32, (toks, toks), 0) < lax.broadcasted_iota(jnp.int32, (toks, toks), 1)
    same = lax.broadcasted_iota(jnp.int32, (toks, toks), 0) == lax.broadcasted_iota(jnp.int32, (toks, toks), 1)
    over = (((0,), (0,)), ((), ()))
    earlier = lax.dot_general(named, jnp.where(before, 1.0, 0.0), over, preferred_element_type=F32)
    chosen = lax.dot_general(named, jnp.where(same, 1.0, 0.0), over, preferred_element_type=F32)
    ranks[z] = jnp.where(chosen > 0.5, earlier, -1.0)
    mine = jnp.dot(tok_ref[...], router_ref[...], preferred_element_type=F32)
    mine = jnp.concatenate([mine, jnp.zeros((toks, 128 - experts), F32)], axis=1)
    logits[q_own] = mine.T[:experts]

    sem = pltpu.get_barrier_semaphore()
    for d in range(1, n):
        pl.semaphore_signal(sem, inc=1, device_id={"expert": lax.rem(z + d, n)}, device_id_type=MESH)
    for d, e in peers:
        target = {"helper": lax.rem(x + d, h), "sub": lax.rem(c + e, s)}
        pl.semaphore_signal(sem, inc=1, device_id=target, device_id_type=MESH)
    pl.semaphore_wait(sem, n - 1 + len(peers))

    for d, e in peers:
        logit_copy(d, e).start()
    for d in range(1, n):
        rank_copy(d).start()
    for k in range(min(AHEAD, chunks)):
        own(k)

    acc[...] = jnp.zeros_like(acc)
    part[...] = jnp.zeros_like(part)
    for d, e in peers:
        q = lax.rem(x + d, h) * s + lax.rem(c + e, s)
        remote(logits.at[q], logits.at[q], l_send.at[0, 0], l_recv.at[q], {"sub": other}).wait_recv()
    total = logits[0]
    for q in range(1, h * s):
        total = total + logits[q]
    zloss_ref[...] = jnp.square(jnp.log(jnp.sum(jnp.exp(total), axis=0, keepdims=True)))
    affinity = jnp.where(ranks[z] >= 0.0, 1.0 / (1.0 + jnp.exp(-total)), 0.0)
    gates[z] = (2.5 * affinity / jnp.sum(affinity, axis=0, keepdims=True)).astype(BF16).astype(F32)
    for d in range(1, n):
        gate_copy(d).start()
    for d in range(1, n):
        zz = lax.rem(z + n - d, n)
        remote(ranks.at[zz], ranks.at[zz], r_send.at[0], r_recv.at[zz], {"sub": other}).wait_recv()
    slot_ids = lax.broadcasted_iota(jnp.int32, (CAP, toks), 0).astype(F32)
    for b in range(n):
        for l in range(local):
            line = ranks[b, pl.ds(z * local + l, 1), :]
            places[b, l * CAP:(l + 1) * CAP, :] = jnp.where(slot_ids == line, 1.0, 0.0)

    def compute(k):
        slot = lax.rem(k, SLOTS)
        for q in range(h * s):
            parts = []
            for p in range(n):
                b = lax.rem(z + 1 + p, n)
                parts.append(
                    jnp.dot(places[b].astype(BF16), tokbuf[k, q, b], preferred_element_type=F32)
                )
            for l in range(local):
                stack = jnp.concatenate([p[l * CAP:(l + 1) * CAP] for p in parts], axis=0)
                rows[l, :, q * width:(q + 1) * width] = stack.astype(BF16)
        for w in weights(k, slot):
            w.wait()

        def one(l, carry):
            for m in range(2):
                acc[m, l] += jnp.dot(
                    rows[l], wbuf[slot, m, l].reshape(h * s * width, ff), preferred_element_type=F32
                )

            @pl.when(k == chunks - 1)
            def _():
                for f in range(2):
                    gate = acc[0, l, f * half:(f + 1) * half]
                    up = acc[1, l, f * half:(f + 1) * half]
                    hbuf[f, l, q_own] = (gate / (1.0 + jnp.exp(-gate)) * up).astype(BF16)
                hid_start(0, l)

            return carry

        lax.fori_loop(0, local, one, 0)

        @pl.when(k + SLOTS < chunks)
        def _():
            for w in weights(k + SLOTS, slot):
                w.start()

    def step(t, carry):
        @pl.when(t + AHEAD < chunks)
        def _():
            own(t + AHEAD)

        @pl.when(t < chunks)
        def _():
            for d in range(1, n):
                zz = lax.rem(z + n - d, n)
                copy(t, q_own, zz, send_z.at[t, 0], {"sub": other}).wait_recv()
                for e in range(1, h):
                    to_x(t, zz, e).start()
                to_s(t, x, zz).start()

        @pl.when(t >= 2)
        def _():
            k = t - 2
            for zz in range(n):
                for xx in range(h):
                    copy(k, xx * s + other, zz, send_z.at[k, 0], {"sub": other}).wait_recv()
            compute(k)

        @pl.when((t >= 1) & (t <= chunks))
        def _():
            k = t - 1
            for d in range(0, n):
                zz = lax.rem(z + n - d, n)
                for e in range(1, h):
                    xx = lax.rem(x + e, h)
                    copy(k, xx * s + c, zz, send_z.at[k, 0], {"sub": other}).wait_recv()
                    to_s(k, xx, zz).start()

        return carry

    lax.fori_loop(0, chunks + 2, step, 0)
    for l in range(local):
        hid_start(1, l)

    for d in range(1, n):
        zz = lax.rem(z + n - d, n)
        remote(gates.at[zz], gates.at[zz], g_send.at[0], g_recv.at[zz], {"sub": other}).wait_recv()
    blank = jnp.zeros((CAP, toks), F32)
    padded = -(-half // 128) * 128
    for f in range(2):
        for l in range(local):
            lines = []
            for i in range(nh):
                b = lax.rem(z + 1 + f * nh + i, n)
                at = pl.ds(z * local + l, 1)
                block = jnp.where(slot_ids == ranks[b, at, :], gates[b, at, :], 0.0)
                lines.append(jnp.concatenate([block if j == i else blank for j in range(nh)], axis=1))
            if padded > half:
                lines.append(jnp.zeros((padded - half, nh * toks), F32))
            table[f, l] = jnp.concatenate(lines, axis=0).T[:, :half].astype(BF16)

    def hid_forward(i):
        f, l = i // local, lax.rem(i, local)
        for e in range(1, h):
            xx = lax.rem(x + e, h)
            hid_copy(f, l, xx * s + c, h_send_x.at[f, l, 0], {"sub": other}).wait_recv()
            hid_s(f, l, xx).start()

    hid_forward(jnp.int32(0))

    def item(i, carry):
        f, l = i // local, lax.rem(i, local)

        @pl.when(i + 1 < items)
        def _():
            hid_forward(i + 1)

        for xx in range(h):
            hid_copy(f, l, xx * s + other, h_send_x.at[f, l, 0], {"sub": other}).wait_recv()
        slot = lax.rem(i, d_slots)
        if local > d_slots:
            down(l, slot).wait()
        else:
            @pl.when(i < local)
            def _():
                down(l, slot).wait()

        full = jnp.concatenate([hbuf[f, l, q] for q in range(h * s)], axis=1)
        for j in range(chunks):
            cols = slice(j * width, (j + 1) * width)
            answer = jnp.dot(full, dbuf[slot, :, cols], preferred_element_type=F32)
            part[f, :, cols] += jnp.dot(table[f, l], answer.astype(BF16), preferred_element_type=F32)

        if local > d_slots:
            @pl.when(i + d_slots < items)
            def _():
                down(lax.rem(i + d_slots, local), slot).start()

        for f_done in range(2):
            @pl.when(i == (f_done + 1) * local - 1)
            def _():
                for p in range(f_done * nh, min((f_done + 1) * nh, n - 1)):
                    at = (p - f_done * nh) * toks
                    sendbuf[p] = part[f_done, at:at + toks].astype(BF16)
                    back(p).start()

        return carry

    lax.fori_loop(0, items, item, 0)

    for p in range(n - 1):
        back(p).wait_recv()
    result = part[1, (nh - 1) * toks:]
    for p in range(n - 1):
        result = result + recvbuf[p].astype(F32)
    out_ref[...] = result.astype(BF16)

    def drain(k, carry):
        for d in range(1, n):
            to_z(k, d).wait_send()
        for zz in range(n):
            for d in range(1, h):
                to_x(k, zz, d).wait_send()
            for xx in range(h):
                to_s(k, xx, zz).wait_send()
        return carry

    lax.fori_loop(0, chunks, drain, 0)

    def drain_hidden(l, carry):
        for f in range(2):
            for d in range(1, h):
                hid_x(f, l, d).wait_send()
            for xx in range(h):
                hid_s(f, l, xx).wait_send()
        return carry

    lax.fori_loop(0, local, drain_hidden, 0)
    for d in range(1, n):
        rank_copy(d).wait_send()
        gate_copy(d).wait_send()
        back(d - 1).wait_send()
    for d, e in peers:
        logit_copy(d, e).wait_send()


def body(tokens, routes, router_weight, gate_weight, up_weight, down_weight):
    n, h, s = (lax.axis_size(a) for a in ("expert", "helper", "sub"))
    experts = router_weight.shape[1]
    local, wide, ff = gate_weight.shape
    toks, own = tokens.shape
    width = own // CHUNKS
    q = h * s
    half = n // 2 * CAP
    shape = (local, q, CHUNKS, width, ff)
    d_slots = min(local, D_SLOTS)
    dims = (n, h, s, local, CHUNKS, width, ff, experts, d_slots)
    dma = pltpu.SemaphoreType.DMA
    vmem = pl.BlockSpec(memory_space=pltpu.VMEM)
    hbm = pl.BlockSpec(memory_space=pl.ANY)
    mixed, zloss = pl.pallas_call(
        functools.partial(layer_kernel, dims),
        out_shape=(
            jax.ShapeDtypeStruct((toks, own), BF16),
            jax.ShapeDtypeStruct((1, toks), F32),
        ),
        in_specs=[vmem, vmem, vmem, hbm, hbm, hbm],
        out_specs=(vmem, vmem),
        scratch_shapes=[
            pltpu.VMEM((CHUNKS, q, n, toks, width), BF16),
            pltpu.VMEM((SLOTS, 2, local, q, width, ff), BF16),
            pltpu.VMEM((d_slots, q * ff, own), BF16),
            pltpu.VMEM((local, n * CAP, q * width), BF16),
            pltpu.VMEM((2, local, n * CAP, ff), F32),
            pltpu.VMEM((n, local * CAP, toks), F32),
            pltpu.VMEM((2, local, n // 2 * toks, half), BF16),
            pltpu.VMEM((n, experts, toks), F32),
            pltpu.VMEM((n, experts, toks), F32),
            pltpu.VMEM((q, experts, toks), F32),
            pltpu.VMEM((2, local, q, half, ff), BF16),
            pltpu.VMEM((2, n // 2 * toks, own), F32),
            pltpu.VMEM((n - 1, toks, own), BF16),
            pltpu.VMEM((n - 1, toks, own), BF16),
            dma((CHUNKS, q, n)),
            dma((CHUNKS, n - 1)),
            dma((CHUNKS, n, h - 1)),
            dma((CHUNKS, h, n)),
            dma((SLOTS, 2)),
            dma((d_slots,)),
            dma((n - 1,)),
            dma((n,)),
            dma((n - 1,)),
            dma((n,)),
            dma((h, s)),
            dma((q,)),
            dma((2, local, q)),
            dma((2, local, h - 1)),
            dma((2, local, h)),
            dma((n - 1,)),
            dma((n - 1,)),
        ],
        compiler_params=pltpu.CompilerParams(
            collective_id=0, has_side_effects=True, vmem_limit_bytes=VMEM_LIMIT
        ),
        cost_estimate=pl.CostEstimate(
            flops=6 * local * n * CAP * wide * ff,
            bytes_accessed=6 * local * wide * ff,
            transcendentals=local * n * CAP * ff,
        ),
        name="expert_layer",
    )(
        tokens, routes, router_weight,
        gate_weight.reshape(shape), up_weight.reshape(shape), down_weight,
    )
    return mixed, zloss.reshape(toks)


def solution(mesh):
    placed = (
        P(("groups", "expert"), ("helper", "sub")),
        P(("groups", "expert"), None),
        P(("helper", "sub"), None),
        P("expert", None, ("helper", "sub")),
        P("expert", None, ("helper", "sub")),
        P("expert", None, ("helper", "sub")),
    )
    return jax.shard_map(
        body,
        mesh=mesh,
        in_specs=placed,
        out_specs=(P(("groups", "expert"), ("helper", "sub")), P(("groups", "expert"))),
        check_vma=False,
    )
```

```python
import functools

import jax
import jax.numpy as jnp
from jax import lax
from jax.experimental import pallas as pl
from jax.experimental.pallas import tpu as pltpu
from jax.sharding import PartitionSpec as P

CAP = 72
CHUNKS = 7
AHEAD = 3
SLOTS = 2
D_SLOTS = 2
VMEM_LIMIT = 62 * 1024 * 1024
MESH = pl.DeviceIdType.MESH
F32 = jnp.float32
BF16 = jnp.bfloat16


def layer_kernel(
    dims, tok_ref, routes_ref, router_ref, gate_hbm, up_hbm, down_hbm, out_ref, zloss_ref,
    tokbuf, wbuf, dbuf, rows, acc, places, table, ranks, gates, logits, hbuf, part, sendbuf, recvbuf,
    recv, send_z, send_x, send_s, w_sem, d_sem, r_send, r_recv, g_send, g_recv, l_send, l_recv,
    h_recv, h_send_x, h_send_s, p_send, p_recv,
):
    n, h, s, local, chunks, width, ff, experts, d_slots = dims
    z, x, c = lax.axis_index("expert"), lax.axis_index("helper"), lax.axis_index("sub")
    other = 1 - c
    q_own = x * s + c
    toks = tok_ref.shape[0]
    nh = n // 2
    half = nh * CAP
    items = 2 * local

    def weights(k, slot):
        return (
            pltpu.make_async_copy(gate_hbm.at[:, :, k], wbuf.at[slot, 0], w_sem.at[slot, 0]),
            pltpu.make_async_copy(up_hbm.at[:, :, k], wbuf.at[slot, 1], w_sem.at[slot, 1]),
        )

    def down(l, slot):
        return pltpu.make_async_copy(down_hbm.at[l], dbuf.at[slot], d_sem.at[slot])

    def remote(src, dst, send, got, target):
        return pltpu.make_async_remote_copy(
            src_ref=src, dst_ref=dst, send_sem=send, recv_sem=got,
            device_id=target, device_id_type=MESH,
        )

    def copy(k, q, zz, send, target):
        ref = tokbuf.at[k, q, zz]
        return remote(ref, ref, send, recv.at[k, q, zz], target)

    def to_z(k, d):
        return copy(k, q_own, z, send_z.at[k, d - 1], {"expert": lax.rem(z + d, n)})

    def to_x(k, zz, d):
        return copy(k, q_own, zz, send_x.at[k, zz, d - 1], {"helper": lax.rem(x + d, h)})

    def to_s(k, xx, zz):
        return copy(k, xx * s + c, zz, send_s.at[k, xx, zz], {"sub": other})

    def rank_copy(d):
        ref = ranks.at[z]
        return remote(ref, ref, r_send.at[d - 1], r_recv.at[z], {"expert": lax.rem(z + d, n)})

    def gate_copy(d):
        ref = gates.at[z]
        return remote(ref, ref, g_send.at[d - 1], g_recv.at[z], {"expert": lax.rem(z + d, n)})

    def logit_copy(d, e):
        ref = logits.at[q_own]
        target = {"helper": lax.rem(x + d, h), "sub": lax.rem(c + e, s)}
        return remote(ref, ref, l_send.at[d, e], l_recv.at[q_own], target)

    peers = [(d, e) for d in range(h) for e in range(s) if d or e]

    def hid_copy(f, l, q, send, target):
        ref = hbuf.at[f, l, q]
        return remote(ref, ref, send, h_recv.at[f, l, q], target)

    def hid_x(f, l, d):
        return hid_copy(f, l, q_own, h_send_x.at[f, l, d - 1], {"helper": lax.rem(x + d, h)})

    def hid_s(f, l, xx):
        return hid_copy(f, l, xx * s + c, h_send_s.at[f, l, xx], {"sub": other})

    def hid_start(f, l):
        for d in range(1, h):
            hid_x(f, l, d).start()
        hid_s(f, l, x).start()

    def back(p):
        return remote(
            sendbuf.at[p], recvbuf.at[p], p_send.at[p], p_recv.at[p],
            {"expert": lax.rem(z + 1 + p, n)},
        )

    def own(k):
        for d in range(1, n):
            to_z(k, d).start()
        for d in range(1, h):
            to_x(k, z, d).start()
        to_s(k, x, z).start()

    for k in range(SLOTS):
        for w in weights(k, k):
            w.start()
    for l in range(min(local, d_slots)):
        down(l, l).start()
    for k in range(chunks):
        tokbuf[k, q_own, z] = tok_ref[:, k * width:(k + 1) * width]

    ids = lax.broadcasted_iota(jnp.int32, (toks, experts), 1)
    named = jnp.zeros((toks, experts), F32)
    for k in range(routes_ref.shape[1]):
        named = named + jnp.where(routes_ref[:, k:k + 1] == ids, 1.0, 0.0)
    before = lax.broadcasted_iota(jnp.int32, (toks, toks), 0) < lax.broadcasted_iota(jnp.int32, (toks, toks), 1)
    same = lax.broadcasted_iota(jnp.int32, (toks, toks), 0) == lax.broadcasted_iota(jnp.int32, (toks, toks), 1)
    over = (((0,), (0,)), ((), ()))
    earlier = lax.dot_general(named, jnp.where(before, 1.0, 0.0), over, preferred_element_type=F32)
    chosen = lax.dot_general(named, jnp.where(same, 1.0, 0.0), over, preferred_element_type=F32)
    ranks[z] = jnp.where(chosen > 0.5, earlier, -1.0)
    mine = jnp.dot(tok_ref[...], router_ref[...], preferred_element_type=F32)
    mine = jnp.concatenate([mine, jnp.zeros((toks, 128 - experts), F32)], axis=1)
    logits[q_own] = mine.T[:experts]

    sem = pltpu.get_barrier_semaphore()
    for d in range(1, n):
        pl.semaphore_signal(sem, inc=1, device_id={"expert": lax.rem(z + d, n)}, device_id_type=MESH)
    for d, e in peers:
        target = {"helper": lax.rem(x + d, h), "sub": lax.rem(c + e, s)}
        pl.semaphore_signal(sem, inc=1, device_id=target, device_id_type=MESH)
    pl.semaphore_wait(sem, n - 1 + len(peers))

    for d, e in peers:
        logit_copy(d, e).start()
    for d in range(1, n):
        rank_copy(d).start()
    for k in range(min(AHEAD, chunks)):
        own(k)

    acc[...] = jnp.zeros_like(acc)
    part[...] = jnp.zeros_like(part)
    for d, e in peers:
        q = lax.rem(x + d, h) * s + lax.rem(c + e, s)
        remote(logits.at[q], logits.at[q], l_send.at[0, 0], l_recv.at[q], {"sub": other}).wait_recv()
    total = logits[0]
    for q in range(1, h * s):
        total = total + logits[q]
    zloss_ref[...] = jnp.square(jnp.log(jnp.sum(jnp.exp(total), axis=0, keepdims=True)))
    affinity = jnp.where(ranks[z] >= 0.0, 1.0 / (1.0 + jnp.exp(-total)), 0.0)
    gates[z] = (2.5 * affinity / jnp.sum(affinity, axis=0, keepdims=True)).astype(BF16).astype(F32)
    for d in range(1, n):
        gate_copy(d).start()
    for d in range(1, n):
        zz = lax.rem(z + n - d, n)
        remote(ranks.at[zz], ranks.at[zz], r_send.at[0], r_recv.at[zz], {"sub": other}).wait_recv()
    slot_ids = lax.broadcasted_iota(jnp.int32, (CAP, toks), 0).astype(F32)
    for b in range(n):
        for l in range(local):
            line = ranks[b, pl.ds(z * local + l, 1), :]
            places[b, l * CAP:(l + 1) * CAP, :] = jnp.where(slot_ids == line, 1.0, 0.0)

    def compute(k):
        slot = lax.rem(k, SLOTS)
        for q in range(h * s):
            parts = []
            for p in range(n):
                b = lax.rem(z + 1 + p, n)
                parts.append(
                    jnp.dot(places[b].astype(BF16), tokbuf[k, q, b], preferred_element_type=F32)
                )
            for l in range(local):
                stack = jnp.concatenate([p[l * CAP:(l + 1) * CAP] for p in parts], axis=0)
                rows[l, :, q * width:(q + 1) * width] = stack.astype(BF16)
        for w in weights(k, slot):
            w.wait()

        def one(l, carry):
            for m in range(2):
                acc[m, l] += jnp.dot(
                    rows[l], wbuf[slot, m, l].reshape(h * s * width, ff), preferred_element_type=F32
                )

            @pl.when(k == chunks - 1)
            def _():
                for f in range(2):
                    gate = acc[0, l, f * half:(f + 1) * half]
                    up = acc[1, l, f * half:(f + 1) * half]
                    hbuf[f, l, q_own] = (gate / (1.0 + jnp.exp(-gate)) * up).astype(BF16)
                hid_start(0, l)

            return carry

        lax.fori_loop(0, local, one, 0)

        @pl.when(k + SLOTS < chunks)
        def _():
            for w in weights(k + SLOTS, slot):
                w.start()

    def step(t, carry):
        @pl.when(t + AHEAD < chunks)
        def _():
            own(t + AHEAD)

        @pl.when(t < chunks)
        def _():
            for d in range(1, n):
                zz = lax.rem(z + n - d, n)
                copy(t, q_own, zz, send_z.at[t, 0], {"sub": other}).wait_recv()
                for e in range(1, h):
                    to_x(t, zz, e).start()
                to_s(t, x, zz).start()

        @pl.when(t >= 2)
        def _():
            k = t - 2
            for zz in range(n):
                for xx in range(h):
                    copy(k, xx * s + other, zz, send_z.at[k, 0], {"sub": other}).wait_recv()
            compute(k)

        @pl.when((t >= 1) & (t <= chunks))
        def _():
            k = t - 1
            for d in range(0, n):
                zz = lax.rem(z + n - d, n)
                for e in range(1, h):
                    xx = lax.rem(x + e, h)
                    copy(k, xx * s + c, zz, send_z.at[k, 0], {"sub": other}).wait_recv()
                    to_s(k, xx, zz).start()

        return carry

    lax.fori_loop(0, chunks + 2, step, 0)
    for l in range(local):
        hid_start(1, l)

    for d in range(1, n):
        zz = lax.rem(z + n - d, n)
        remote(gates.at[zz], gates.at[zz], g_send.at[0], g_recv.at[zz], {"sub": other}).wait_recv()
    blank = jnp.zeros((CAP, toks), F32)
    padded = -(-half // 128) * 128
    for f in range(2):
        for l in range(local):
            lines = []
            for i in range(nh):
                b = lax.rem(z + 1 + f * nh + i, n)
                at = pl.ds(z * local + l, 1)
                block = jnp.where(slot_ids == ranks[b, at, :], gates[b, at, :], 0.0)
                lines.append(jnp.concatenate([block if j == i else blank for j in range(nh)], axis=1))
            if padded > half:
                lines.append(jnp.zeros((padded - half, nh * toks), F32))
            table[f, l] = jnp.concatenate(lines, axis=0).T[:, :half].astype(BF16)

    def hid_forward(i):
        f, l = i // local, lax.rem(i, local)
        for e in range(1, h):
            xx = lax.rem(x + e, h)
            hid_copy(f, l, xx * s + c, h_send_x.at[f, l, 0], {"sub": other}).wait_recv()
            hid_s(f, l, xx).start()

    hid_forward(jnp.int32(0))

    def item(i, carry):
        f, l = i // local, lax.rem(i, local)

        @pl.when(i + 1 < items)
        def _():
            hid_forward(i + 1)

        for xx in range(h):
            hid_copy(f, l, xx * s + other, h_send_x.at[f, l, 0], {"sub": other}).wait_recv()
        slot = lax.rem(i, d_slots)
        if local > d_slots:
            down(l, slot).wait()
        else:
            @pl.when(i < local)
            def _():
                down(l, slot).wait()

        full = jnp.concatenate([hbuf[f, l, q] for q in range(h * s)], axis=1)
        for j in range(chunks):
            cols = slice(j * width, (j + 1) * width)
            answer = jnp.dot(full, dbuf[slot, :, cols], preferred_element_type=F32)
            part[f, :, cols] += jnp.dot(table[f, l], answer.astype(BF16), preferred_element_type=F32)

        if local > d_slots:
            @pl.when(i + d_slots < items)
            def _():
                down(lax.rem(i + d_slots, local), slot).start()

        for f_done in range(2):
            @pl.when(i == (f_done + 1) * local - 1)
            def _():
                for p in range(f_done * nh, min((f_done + 1) * nh, n - 1)):
                    at = (p - f_done * nh) * toks
                    sendbuf[p] = part[f_done, at:at + toks].astype(BF16)
                    back(p).start()

        return carry

    lax.fori_loop(0, items, item, 0)

    for p in range(n - 1):
        back(p).wait_recv()
    result = part[1, (nh - 1) * toks:]
    for p in range(n - 1):
        result = result + recvbuf[p].astype(F32)
    out_ref[...] = result.astype(BF16)

    def drain(k, carry):
        for d in range(1, n):
            to_z(k, d).wait_send()
        for zz in range(n):
            for d in range(1, h):
                to_x(k, zz, d).wait_send()
            for xx in range(h):
                to_s(k, xx, zz).wait_send()
        return carry

    lax.fori_loop(0, chunks, drain, 0)

    def drain_hidden(l, carry):
        for f in range(2):
            for d in range(1, h):
                hid_x(f, l, d).wait_send()
            for xx in range(h):
                hid_s(f, l, xx).wait_send()
        return carry

    lax.fori_loop(0, local, drain_hidden, 0)
    for d in range(1, n):
        rank_copy(d).wait_send()
        gate_copy(d).wait_send()
        back(d - 1).wait_send()
    for d, e in peers:
        logit_copy(d, e).wait_send()


def body(tokens, routes, router_weight, gate_weight, up_weight, down_weight):
    n, h, s = (lax.axis_size(a) for a in ("expert", "helper", "sub"))
    experts = router_weight.shape[1]
    local, wide, ff = gate_weight.shape
    toks, own = tokens.shape
    width = own // CHUNKS
    q = h * s
    half = n // 2 * CAP
    shape = (local, q, CHUNKS, width, ff)
    d_slots = min(local, D_SLOTS)
    dims = (n, h, s, local, CHUNKS, width, ff, experts, d_slots)
    dma = pltpu.SemaphoreType.DMA
    vmem = pl.BlockSpec(memory_space=pltpu.VMEM)
    hbm = pl.BlockSpec(memory_space=pl.ANY)
    mixed, zloss = pl.pallas_call(
        functools.partial(layer_kernel, dims),
        out_shape=(
            jax.ShapeDtypeStruct((toks, own), BF16),
            jax.ShapeDtypeStruct((1, toks), F32),
        ),
        in_specs=[vmem, vmem, vmem, hbm, hbm, hbm],
        out_specs=(vmem, vmem),
        scratch_shapes=[
            pltpu.VMEM((CHUNKS, q, n, toks, width), BF16),
            pltpu.VMEM((SLOTS, 2, local, q, width, ff), BF16),
            pltpu.VMEM((d_slots, q * ff, own), BF16),
            pltpu.VMEM((local, n * CAP, q * width), BF16),
            pltpu.VMEM((2, local, n * CAP, ff), F32),
            pltpu.VMEM((n, local * CAP, toks), F32),
            pltpu.VMEM((2, local, n // 2 * toks, half), BF16),
            pltpu.VMEM((n, experts, toks), F32),
            pltpu.VMEM((n, experts, toks), F32),
            pltpu.VMEM((q, experts, toks), F32),
            pltpu.VMEM((2, local, q, half, ff), BF16),
            pltpu.VMEM((2, n // 2 * toks, own), F32),
            pltpu.VMEM((n - 1, toks, own), BF16),
            pltpu.VMEM((n - 1, toks, own), BF16),
            dma((CHUNKS, q, n)),
            dma((CHUNKS, n - 1)),
            dma((CHUNKS, n, h - 1)),
            dma((CHUNKS, h, n)),
            dma((SLOTS, 2)),
            dma((d_slots,)),
            dma((n - 1,)),
            dma((n,)),
            dma((n - 1,)),
            dma((n,)),
            dma((h, s)),
            dma((q,)),
            dma((2, local, q)),
            dma((2, local, h - 1)),
            dma((2, local, h)),
            dma((n - 1,)),
            dma((n - 1,)),
        ],
        compiler_params=pltpu.CompilerParams(
            collective_id=0, has_side_effects=True, vmem_limit_bytes=VMEM_LIMIT
        ),
        cost_estimate=pl.CostEstimate(
            flops=6 * local * n * CAP * wide * ff,
            bytes_accessed=6 * local * wide * ff,
            transcendentals=local * n * CAP * ff,
        ),
        name="expert_layer",
    )(
        tokens, routes, router_weight,
        gate_weight.reshape(shape), up_weight.reshape(shape), down_weight,
    )
    return mixed, zloss.reshape(toks)


def solution(mesh):
    placed = (
        P(("groups", "expert"), ("helper", "sub")),
        P(("groups", "expert"), None),
        P(("helper", "sub"), None),
        P("expert", None, ("helper", "sub")),
        P("expert", None, ("helper", "sub")),
        P("expert", None, ("helper", "sub")),
    )
    return jax.shard_map(
        body,
        mesh=mesh,
        in_specs=placed,
        out_specs=(P(("groups", "expert"), ("helper", "sub")), P(("groups", "expert"))),
        check_vma=False,
    )
```
